32 devices in a mesh: colony: 8 (over z, y), fsdp: 4 (over x, core).
Axes of the slice: x: 2, y: 2, z: 4, core: 2. Of those that a mesh axis runs over, the one named last changes fastest.
Arguments:
- hidden_states: bfloat16 [8, 512, 4096], P('colony', 'fsdp'), may hold values from -40 to 40
- norm_gain: float32 [4096], replicated, may hold values from 0.25 to 1.75
- gate_weight: bfloat16 [4096, 7168], P(None, 'fsdp'), may hold values from -0.09375 to 0.09375
- up_weight: bfloat16 [4096, 7168], P(None, 'fsdp'), may hold values from -0.09375 to 0.09375
- hidden_grad: bfloat16 [8, 512, 7168], P('colony', 'fsdp'), may hold values from -2 to 2
- byz_order: int32 [8], replicated, may hold values from 0 to 7, each once
- byz_scale: float32 [3], replicated, may hold values from 2 to 6
Outputs:
- median_gate: float32 [4096, 7168], P('colony', 'fsdp')
- median_up: float32 [4096, 7168], P('colony', 'fsdp')
The draws below stay inside these ranges and needn't reach their ends.
All inputs are finite; a program needn't handle non-finite values.
Results may differ from the reference program's by a relative error of at most 0.002.
The reference program's roundings to bfloat16 on the way (of `normed` and `grads`) count: a program that leaves them out, or rounds other values in their place, can miss the bound.
Values may be sent and summed in bfloat16 or wider, within the bound.
No kernel may reach another device: no remote copies, remote signals or barrier semaphores. Data moves between devices by JAX's collectives and lax.ppermute only.
A program may use at most 192 MiB of HBM per device.

```python
import math
import jax
import jax.numpy as jnp
from jax import lax

D = 4096
FF = 7168
TOK_DEV = 128
NBYZ = 3
ITERS = 3
COL_TOKENS = 512
COLONIES = 8


def draw_hidden_states(key, part):
    key = jax.random.fold_in(key, 5)
    slope_key = jax.random.fold_in(key, 11)
    tilt_key = jax.random.fold_in(key, 13)
    shared_key = jax.random.fold_in(key, 23)
    own_key = jax.random.fold_in(key, 29)
    position = jnp.arange(D, dtype=jnp.float32) / D - 0.5
    slope = jax.random.uniform(slope_key, (1, 1, 1), jnp.float32, -1.0, 1.0)
    tilt = jax.random.uniform(tilt_key, (COLONIES, 1, 1), jnp.float32, -0.3, 0.3)
    span = math.log(9.0)
    shared = jnp.clip(jax.random.normal(shared_key, (1, COL_TOKENS, D), jnp.float32), -4.0, 4.0)
    own = jnp.clip(jax.random.normal(own_key, (COLONIES, COL_TOKENS, D), jnp.float32), -4.0, 4.0)
    mixed = 0.95 * shared + 0.3 * own
    profile = jnp.exp((slope + tilt) * span * position[None, None, :])
    return (mixed * profile).astype(jnp.bfloat16)


def draw_hidden_grad(key, part):
    key = jax.random.fold_in(key, 7)
    shared_key = jax.random.fold_in(key, 31)
    own_key = jax.random.fold_in(key, 37)
    level_key = jax.random.fold_in(key, 41)
    blocks = COL_TOKENS // TOK_DEV
    width = FF // blocks
    level = jnp.exp(jax.random.uniform(level_key, (COLONIES, 1, blocks), jnp.float32, -2.4, 0.0))
    column_block = jnp.arange(FF, dtype=jnp.int32) // width
    column_level = level[:, :, column_block]
    shared = jnp.clip(jax.random.normal(shared_key, (1, COL_TOKENS, FF), jnp.float32), -4.0, 4.0)
    own = jnp.clip(jax.random.normal(own_key, (COLONIES, COL_TOKENS, FF), jnp.float32), -4.0, 4.0)
    mixed = shared + 0.35 * own
    scale = float(COL_TOKENS) ** (-0.5)
    return (mixed * column_level * scale).astype(jnp.bfloat16)


def block_levels(stream_key, extent, shards, smallest, largest):
    level = 1.0
    for axis_at, shards_of in shards:
        steps = jax.random.uniform(jax.random.fold_in(jax.random.fold_in(stream_key, 6), axis_at), (shards_of,), jnp.float32, smallest / len(shards), largest / len(shards))
        level = level * jnp.repeat(jnp.exp(steps), extent[axis_at] // shards_of).reshape((-1,) + (1,) * (len(extent) - 1 - axis_at))
    return level


def scatter_about(stream_key, extent, spread, limit, pieces=(), held_as=jnp.bfloat16):
    values = jax.random.normal(stream_key, extent, jnp.float32) * spread
    if len(pieces) > 0:
        values = block_levels(stream_key, extent, pieces, -0.22, 0.18) * values
    return jnp.clip(values, min=-limit, max=limit).astype(held_as)


def setup_inputs(seed: int = 0) -> dict:
    key_of = jax.random.split(jax.random.key(seed), 8)
    hidden_states = draw_hidden_states(jax.random.fold_in(key_of[7], 71), 0)
    norm_gain = jnp.clip(1.0 + 0.15 * jax.random.normal(key_of[1], (D,), jnp.float32), 0.25, 1.75)
    gate_weight = scatter_about(key_of[2], (D, FF), D ** -0.5, 0.09375, ((1, 4),))
    up_weight = scatter_about(key_of[3], (D, FF), D ** -0.5, 0.09375, ((1, 4),))
    hidden_grad = draw_hidden_grad(jax.random.fold_in(key_of[7], 71), 0)
    byz_order = jax.random.permutation(key_of[5], COLONIES).astype(jnp.int32)
    byz_scale = jnp.clip(jax.random.uniform(key_of[6], (NBYZ,), jnp.float32, 2.0, 6.0), 2.0, 6.0)
    return {"hidden_states": hidden_states, "norm_gain": norm_gain, "gate_weight": gate_weight, "up_weight": up_weight, "hidden_grad": hidden_grad, "byz_order": byz_order, "byz_scale": byz_scale}


def reference(hidden_states, norm_gain, gate_weight, up_weight, hidden_grad, byz_order, byz_scale):

    def one_colony(item):
        states, cotangent = item
        values = states.astype(jnp.float32)
        meansq = lax.optimization_barrier(jnp.mean(values * values, axis=-1, keepdims=True))
        normed = (values * lax.rsqrt(meansq + 1e-05) * norm_gain).astype(jnp.bfloat16)
        gate = jnp.dot(normed, gate_weight, preferred_element_type=jnp.float32)
        up = jnp.dot(normed, up_weight, preferred_element_type=jnp.float32)
        sig = jax.nn.sigmoid(gate)
        back = cotangent.astype(jnp.float32)
        d_up = (back * gate * sig).astype(jnp.bfloat16)
        d_gate = (back * up * sig * (1.0 + gate * (1.0 - sig))).astype(jnp.bfloat16)
        dims = (((0,), (0,)), ((), ()))
        grad_gate = lax.dot_general(normed, d_gate, dims, preferred_element_type=jnp.float32).astype(jnp.bfloat16)
        grad_up = lax.dot_general(normed, d_up, dims, preferred_element_type=jnp.float32).astype(jnp.bfloat16)
        return jnp.stack([grad_gate, grad_up])
    grads = lax.map(one_colony, (hidden_states, hidden_grad))
    colonies = jnp.arange(COLONIES, dtype=jnp.int32)
    hits = byz_order[:NBYZ][:, None] == colonies[None, :]
    factor = 1.0 + lax.optimization_barrier(jnp.sum(jnp.where(hits, -byz_scale[:, None] - 1.0, jnp.float32(0.0)), axis=0))

    def combine(coef):

        def add(total, item):
            grad, weight = item
            return (total + weight * grad.astype(jnp.float32), None)
        total, _ = lax.scan(add, jnp.zeros(grads.shape[1:], jnp.float32), (grads, coef))
        return total
    median = combine(factor / COLONIES)
    for step in range(ITERS):

        def squared(item):
            grad, scale = item
            diff = scale * grad.astype(jnp.float32) - median
            return jnp.sum(diff * diff)
        dist = jnp.sqrt(lax.map(squared, (grads, factor)) + 1e-06)
        weights = 1.0 / dist
        median = combine(weights * factor / jnp.sum(weights))
    return (median[0], median[1])
```

```python
import functools

import jax
import jax.numpy as jnp
from jax import lax
from jax.experimental import pallas as pl
from jax.experimental.pallas import tpu as pltpu
from jax.sharding import PartitionSpec as P

NBYZ = 3
ITERS = 3
LINE = 4
AXES = ("colony", "fsdp")
MIB = 1024 * 1024


def ring_order(count):
    width = count // LINE
    if count % LINE or width % 2:
        return list(range(count))
    order = [(0, 0)]
    for y in range(width):
        column = list(range(1, LINE))
        order += [(z, y) for z in (column if y % 2 == 0 else column[::-1])]
    order += [(0, y) for y in range(width - 1, 0, -1)]
    return [z * width + y for z, y in order]


def slot_shifts(count):
    shifts = [0]
    for step in range(1, count // 2):
        shifts += [step, -step]
    return shifts + [count // 2]


def lane_sums(square):
    rows, lanes = square.shape
    total = square[:, :128]
    for at in range(128, lanes, 128):
        total = total + square[:, at : at + 128]
    return jnp.sum(total.reshape(rows // 8, 8, 128), axis=0)


def colony_kernel(slot, count, parts, share, n_cot, place_of, last, *refs):
    refs = list(refs)
    factor_ref = refs.pop(0)
    slots_ref = refs.pop(0)
    parts_refs = [refs.pop(0) for _ in parts]
    gate_ref, up_ref = refs.pop(0), refs.pop(0)
    cot_refs = [refs.pop(0) for _ in range(n_cot)]
    before = [refs.pop(0) for _ in range(slot)]
    earlier_ref = refs.pop(0) if last else None
    grad_ref = refs.pop(0)
    pair_ref = refs.pop(0) if slot else None
    tokens, rows_t, sems = refs[:3]
    acc = refs[3] if slot else None
    step = pl.program_id(0)
    steps = pl.num_programs(0)
    rows = rows_t.shape[0]

    @pl.when(step == 0)
    def _():
        copies = []
        for at, (ref, pieces) in enumerate(zip(parts_refs, parts)):
            for start, size, target in pieces:
                copies.append(
                    pltpu.make_async_copy(
                        ref.at[pl.ds(start, size)],
                        tokens.at[pl.ds(target, size)],
                        sems.at[len(copies)],
                    )
                )
        for copy in copies:
            copy.start()
        for copy in copies:
            copy.wait()
        first = pl.multiple_of(slots_ref[count] * rows, rows)
        rows_t[...] = tokens[:, pl.ds(first, rows)].T
        if slot:
            acc[...] = jnp.zeros_like(acc)

    gate = jnp.dot(tokens[...], gate_ref[...], preferred_element_type=jnp.float32)
    up = jnp.dot(tokens[...], up_ref[...], preferred_element_type=jnp.float32)
    sig = jax.nn.sigmoid(gate)
    cot = [ref[...] for ref in cot_refs]
    back = (cot[0] if n_cot == 1 else jnp.concatenate(cot, axis=0)).astype(jnp.float32)
    d_up = (back * gate * sig).astype(jnp.bfloat16)
    d_gate = (back * up * sig * (1.0 + gate * (1.0 - sig))).astype(jnp.bfloat16)
    turned = rows_t[...]
    grad_ref[0] = jnp.dot(turned, d_gate, preferred_element_type=jnp.float32).astype(jnp.bfloat16)
    grad_ref[1] = jnp.dot(turned, d_up, preferred_element_type=jnp.float32).astype(jnp.bfloat16)

    if slot:
        scales = [factor_ref[k] for k in range(slot + 1)]
        chunk = 32

        for matrix in range(2):

            def body(at, sums, matrix=matrix):
                span = pl.ds(pl.multiple_of(at * chunk, chunk), chunk)
                mine = scales[slot] * grad_ref[matrix, span, :].astype(jnp.float32)
                out = []
                for k in range(slot):
                    diff = mine - scales[k] * before[k][matrix, span, :].astype(jnp.float32)
                    out.append(sums[k] + lane_sums(diff * diff))
                return tuple(out)

            start = tuple(acc[k] for k in range(slot))
            done = lax.fori_loop(0, rows // chunk, body, start)
            for k in range(slot):
                acc[k] = done[k]

        @pl.when(step == steps - 1)
        def _():
            if not last:
                for k in range(slot):
                    pair_ref[k] = acc[k]
                return
            shape = pair_ref.shape
            row = lax.broadcasted_iota(jnp.int32, shape, 0)
            lane = lax.broadcasted_iota(jnp.int32, shape, 1)
            table = jnp.zeros(shape, jnp.float32)
            at = 0
            for one in range(1, count):
                for two in range(one):
                    part = acc[two] if one == slot else earlier_ref[at]
                    at += 1
                    a, b = slots_ref[one], slots_ref[two]
                    here = ((row == a) & (lane == b)) | ((row == b) & (lane == a))
                    table = table + jnp.where(here, jnp.sum(part), 0.0)
            pair_ref[...] = table


def combine_kernel(count, table_ref, factor_ref, slots_ref, *refs):
    grads = refs[:count]
    gate_out, up_out = refs[count : count + 2]
    coef = refs[count + 2]

    @pl.when(pl.program_id(0) == 0)
    def _():
        table = table_ref[...]
        shape = table.shape
        in_row = lax.broadcasted_iota(jnp.int32, (1, shape[1]), 1) < count
        in_column = lax.broadcasted_iota(jnp.int32, (shape[0], 1), 0) < count
        share_row = jnp.where(in_row, 1.0 / count, 0.0)
        share_column = jnp.where(in_column, 1.0 / count, 0.0)
        for _ in range(ITERS):
            by_row = table * share_row
            near_column = jnp.sum(by_row, axis=1, keepdims=True)
            near_row = jnp.sum(table * share_column, axis=0, keepdims=True)
            half = 0.5 * jnp.sum(near_column * share_column)
            dist_row = jnp.sqrt(jnp.maximum(near_row - half, 0.0) + 1e-06)
            dist_column = jnp.sqrt(jnp.maximum(near_column - half, 0.0) + 1e-06)
            weight_row = jnp.where(in_row, 1.0 / dist_row, 0.0)
            weight_column = jnp.where(in_column, 1.0 / dist_column, 0.0)
            share_row = weight_row / jnp.sum(weight_row)
            share_column = weight_column / jnp.sum(weight_column)
        lane = lax.broadcasted_iota(jnp.int32, (1, shape[1]), 1)
        for k in range(count):
            coef[k] = jnp.sum(jnp.where(lane == slots_ref[k], share_row, 0.0)) * factor_ref[k]

    scales = [coef[k] for k in range(count)]
    rows = gate_out.shape[0]
    chunk = 16
    for matrix, out in ((0, gate_out), (1, up_out)):

        def body(at, carry, matrix=matrix, out=out):
            span = pl.ds(pl.multiple_of(at * chunk, chunk), chunk)
            total = scales[0] * grads[0][matrix, span, :].astype(jnp.float32)
            for k in range(1, count):
                total = total + scales[k] * grads[k][matrix, span, :].astype(jnp.float32)
            out[span, :] = total
            return carry

        lax.fori_loop(0, rows // chunk, body, 0)


def on_device(order, hidden_states, norm_gain, gate_weight, up_weight, hidden_grad, byz_order, byz_scale):
    count, shards = len(order), lax.axis_size("fsdp")
    colony, shard = lax.axis_index("colony"), lax.axis_index("fsdp")
    width = gate_weight.shape[1]
    depth = hidden_states.shape[2]
    share = hidden_states.shape[1]
    half = share // 2
    rows = depth // count
    total_tokens = share * shards
    block = 256 if width % 256 == 0 else 128
    place = {c: at for at, c in enumerate(order)}
    shifts = slot_shifts(count)

    def hop(value, delta):
        pairs = []
        for c in range(count):
            to = order[(place[c] + delta) % count]
            pairs.append((c, to))
        return lax.ppermute(value, "colony", pairs)

    def swap(value, mask):
        return lax.ppermute(value, "fsdp", [(j, j ^ mask) for j in range(shards)])

    def spread(own):
        pieces = {0: own}
        bit = shards // 2
        while bit:
            for m in list(pieces):
                pieces[m | bit] = swap(pieces[m], bit)
            bit //= 2
        return [pieces[m] for m in range(shards)]

    values = hidden_states[0].astype(jnp.float32)
    meansq = jnp.mean(values * values, axis=-1, keepdims=True)
    normed = (values * lax.rsqrt(meansq + 1e-05) * norm_gain).astype(jnp.bfloat16)

    local_grad = hidden_grad[0]
    cuts = []
    for m in range(shards):
        columns = lax.dynamic_slice(local_grad, (0, (shard ^ m) * width), (share, width))
        cuts.append(columns if m == 0 else swap(columns, m))
    cot = jnp.concatenate([c[h * half : (h + 1) * half] for h in range(2) for c in cuts], axis=0)
    mid = total_tokens // 2

    tokens, cots = [None] * count, [None] * count
    tokens[0], cots[0] = spread(normed), [cot]
    ahead = {1: (normed, cot), -1: (normed, cot)}
    slot = 1
    for step in range(1, count // 2):
        for way in (1, -1):
            n, c = ahead[way]
            n, c = hop(n, way), hop(c, way)
            ahead[way] = (n, c)
            tokens[slot], cots[slot] = spread(n), [c]
            slot += 1
    halves = []
    last_cots = []
    for h, way in ((0, 1), (1, -1)):
        n, c = ahead[way]
        halves.append(spread(hop(n[h * half : (h + 1) * half], way)))
        last_cots.append(hop(c[h * mid : (h + 1) * mid], way))
    tokens[slot], cots[slot] = halves[0] + halves[1], last_cots

    ring = jnp.asarray(order, jnp.int32)
    at = jnp.asarray([place[c] for c in range(count)], jnp.int32)[colony]
    held = ring[(at - jnp.asarray(shifts, jnp.int32)) % count]
    slots = jnp.concatenate([held, colony[None].astype(jnp.int32)])
    hits = byz_order[:NBYZ][:, None] == held[None, :]
    factor = 1.0 + jnp.sum(jnp.where(hits, -byz_scale[:, None] - 1.0, jnp.float32(0.0)), axis=0)

    smem = pl.BlockSpec(memory_space=pltpu.SMEM)
    anywhere = pl.BlockSpec(memory_space=pl.ANY)
    table_shape = (max(8, count), 128)
    grads, pairs = [], []
    for k in range(count):
        last = k == count - 1
        if last:
            parts = [[(0, half, (h * shards + m) * half)] for h in range(2) for m in range(shards)]
        else:
            parts = [
                [(h * half, half, (h * shards + m) * half) for h in range(2)] for m in range(shards)
            ]
        column = pl.BlockSpec((depth, block), lambda b: (0, b))
        block_of_grad = pl.BlockSpec((2, rows, block), lambda b: (0, 0, b))
        in_specs = [smem, smem] + [anywhere] * len(parts) + [column, column]
        in_specs += [pl.BlockSpec((c.shape[0], block), lambda b: (0, b)) for c in cots[k]]
        in_specs += [block_of_grad] * k
        operands = [factor, slots, *tokens[k], gate_weight, up_weight, *cots[k], *grads]
        out_shape = [jax.ShapeDtypeStruct((2, rows, width), jnp.bfloat16)]
        out_specs = [block_of_grad]
        scratch = [
            pltpu.VMEM((total_tokens, depth), jnp.bfloat16),
            pltpu.VMEM((rows, total_tokens), jnp.bfloat16),
            pltpu.SemaphoreType.DMA((2 * shards,)),
        ]
        if last:
            earlier = jnp.concatenate(pairs, axis=0)
            operands.append(earlier)
            in_specs.append(pl.BlockSpec(earlier.shape, lambda b: (0, 0, 0)))
            out_shape.append(jax.ShapeDtypeStruct(table_shape, jnp.float32))
            out_specs.append(pl.BlockSpec(table_shape, lambda b: (0, 0)))
        elif k:
            out_shape.append(jax.ShapeDtypeStruct((k, 8, 128), jnp.float32))
            out_specs.append(pl.BlockSpec((k, 8, 128), lambda b: (0, 0, 0)))
        if k:
            scratch.append(pltpu.VMEM((k, 8, 128), jnp.float32))
        flops = 2 * total_tokens * width * 2 * (depth + rows)
        out = pl.pallas_call(
            functools.partial(colony_kernel, k, count, parts, share, len(cots[k]), place, last),
            grid=(width // block,),
            in_specs=in_specs,
            out_specs=out_specs,
            out_shape=out_shape,
            scratch_shapes=scratch,
            compiler_params=pltpu.CompilerParams(vmem_limit_bytes=40 * MIB),
            cost_estimate=pl.CostEstimate(
                flops=flops, bytes_accessed=4 * depth * width, transcendentals=total_tokens * width
            ),
        )(*operands)
        grads.append(out[0])
        if k:
            pairs.append(out[1])

    table = pairs[-1]
    devices = count * shards
    bit = 1
    while bit < devices:
        table = table + lax.ppermute(table, AXES, [(d, d ^ bit) for d in range(devices)])
        bit *= 2

    out_block = pl.BlockSpec((rows, block), lambda b: (0, b))
    return pl.pallas_call(
        functools.partial(combine_kernel, count),
        grid=(width // block,),
        in_specs=[pl.BlockSpec(table_shape, lambda b: (0, 0)), smem, smem]
        + [pl.BlockSpec((2, rows, block), lambda b: (0, 0, b))] * count,
        out_specs=[out_block, out_block],
        out_shape=[jax.ShapeDtypeStruct((rows, width), jnp.float32)] * 2,
        scratch_shapes=[pltpu.SMEM((count,), jnp.float32)],
        compiler_params=pltpu.CompilerParams(vmem_limit_bytes=40 * MIB),
    )(table, factor, slots, *grads)


def solution(mesh):
    placed = (
        P("colony", "fsdp", None),
        P(),
        P(None, "fsdp"),
        P(None, "fsdp"),
        P("colony", "fsdp", None),
        P(),
        P(),
    )
    return jax.shard_map(
        functools.partial(on_device, ring_order(mesh.shape["colony"])),
        mesh=mesh,
        in_specs=placed,
        out_specs=(P("colony", "fsdp"), P("colony", "fsdp")),
        check_vma=False,
    )
```

```python
import functools

import jax
import jax.numpy as jnp
from jax import lax
from jax.experimental import pallas as pl
from jax.experimental.pallas import tpu as pltpu
from jax.sharding import PartitionSpec as P

NBYZ = 3
ITERS = 3
LINE = 4
AXES = ("colony", "fsdp")
VMEM = 28 * 1024 * 1024


def ring_order(count):
    width = count // LINE
    if count % LINE or width % 2:
        return list(range(count))
    order = [(0, 0)]
    for y in range(width):
        column = list(range(1, LINE))
        order += [(z, y) for z in (column if y % 2 == 0 else column[::-1])]
    order += [(0, y) for y in range(width - 1, 0, -1)]
    return [z * width + y for z, y in order]


def slot_shifts(count):
    shifts = [0]
    for step in range(1, count // 2):
        shifts += [step, -step]
    return shifts + [count // 2]


def exact_dot(left, right):
    return jnp.dot(
        left, right, precision=lax.Precision.HIGHEST, preferred_element_type=jnp.float32
    )


def one_hot(shape, axis, sub, slots_ref, slots):
    piece = lax.broadcasted_iota(jnp.int32, shape, axis)
    colony = lax.broadcasted_iota(jnp.int32, shape, 1 - axis)
    result = jnp.zeros(shape, jnp.float32)
    for slot in slots:
        hit = (piece >= slot * sub) & (piece < (slot + 1) * sub) & (colony == slots_ref[slot])
        result = jnp.where(hit, 1.0, result)
    return result


def colony_kernel(slots, count, parts, n_parts, n_cot, *refs):
    refs = list(refs)
    last = slots[-1] == count - 1
    slots_ref = refs.pop(0)
    parts_refs = [refs.pop(0) for _ in range(n_parts)]
    gate_ref, up_ref = refs.pop(0), refs.pop(0)
    cot_refs = [[refs.pop(0) for _ in range(n_cot)] for _ in slots]
    before = [refs.pop(0) for _ in range(slots[0])] if last else []
    grad_refs = [refs.pop(0) for _ in slots]
    table_ref = refs.pop(0) if last else None
    tokens, rows_t, sems = refs[:3]
    gram = refs[3] if last else None
    step = pl.program_id(0)
    rows = rows_t.shape[1]

    copies = []
    for at, part in enumerate(parts):
        copies.append([])
        for which, start, size, target in part:
            copies[at].append(
                pltpu.make_async_copy(
                    parts_refs[which].at[pl.ds(start, size)],
                    tokens.at[at, pl.ds(target, size)],
                    sems.at[at, len(copies[at])],
                )
            )

    def arrive(at):
        for copy in copies[at]:
            copy.wait()
        if at + 1 < len(slots):
            for copy in copies[at + 1]:
                copy.start()
        first = pl.multiple_of(slots_ref[count] * rows, rows)
        rows_t[at] = tokens[at, :, pl.ds(first, rows)].T

    def gradients(at):
        gate = jnp.dot(tokens[at], gate_ref[...], preferred_element_type=jnp.float32)
        up = jnp.dot(tokens[at], up_ref[...], preferred_element_type=jnp.float32)
        sig = jax.nn.sigmoid(gate)
        cot = [ref[...] for ref in cot_refs[at]]
        back = (cot[0] if n_cot == 1 else jnp.concatenate(cot, axis=0)).astype(jnp.float32)
        d_up = (back * gate * sig).astype(jnp.bfloat16)
        d_gate = (back * up * sig * (1.0 + gate * (1.0 - sig))).astype(jnp.bfloat16)
        for matrix, delta in ((0, d_gate), (1, d_up)):
            grad_refs[at][matrix] = jnp.dot(
                rows_t[at], delta, preferred_element_type=jnp.float32
            ).astype(jnp.bfloat16)

    def products():
        every = before + grad_refs
        sub = gram.shape[0] // count
        wide = 8

        def add(at, carry):
            cut = []
            for part in range(wide):
                span = pl.ds(pl.multiple_of((at * wide + part) * sub, sub), sub)
                for matrix in range(2):
                    pieces = [ref[matrix, span, :] for ref in every]
                    cut.append(jnp.concatenate(pieces, axis=0))
            side = jnp.concatenate(cut, axis=1)
            gram[...] += lax.dot_general(
                side, side, (((1,), (1,)), ((), ())), preferred_element_type=jnp.float32
            )
            return carry

        lax.fori_loop(0, rows // (sub * wide), add, 0)

    @pl.when(step == 0)
    def _():
        for copy in copies[0]:
            copy.start()
        if last:
            gram[...] = jnp.zeros_like(gram)
        for at in range(len(slots)):
            arrive(at)
            gradients(at)

    @pl.when(step > 0)
    def _():
        for at in range(len(slots)):
            gradients(at)

    if last:
        products()

        @pl.when(step == pl.num_programs(0) - 1)
        def _():
            size = gram.shape[0]
            sub = size // count
            row = lax.broadcasted_iota(jnp.int32, gram.shape, 0)
            lane = lax.broadcasted_iota(jnp.int32, gram.shape, 1)
            kept = jnp.where((row & (sub - 1)) == (lane & (sub - 1)), gram[...], 0.0)
            left = one_hot((table_ref.shape[0], size), 1, sub, slots_ref, range(count))
            right = one_hot((size, table_ref.shape[1]), 0, sub, slots_ref, range(count))
            table_ref[...] = exact_dot(exact_dot(left, kept), right)


def combine_kernel(count, table_ref, factors_ref, factor_ref, slots_ref, *refs):
    grads = refs[:count]
    gate_out, up_out = refs[count : count + 2]
    coef = refs[count + 2]

    @pl.when(pl.program_id(0) == 0)
    def _():
        table = table_ref[...] * factors_ref[...]
        shape = table.shape
        row = lax.broadcasted_iota(jnp.int32, shape, 0)
        lane = lax.broadcasted_iota(jnp.int32, shape, 1)
        one = jnp.where(row == lane, 1.0, 0.0)
        in_row = lax.broadcasted_iota(jnp.int32, (1, shape[1]), 1) < count
        in_column = lax.broadcasted_iota(jnp.int32, (shape[0], 1), 0) < count
        share_row = jnp.where(in_row, 1.0 / count, 0.0)
        share_column = jnp.where(in_column, 1.0 / count, 0.0)
        for _ in range(ITERS):
            to_row = jnp.sum(table * share_column, axis=0, keepdims=True)
            to_column = jnp.sum(table * share_row, axis=1, keepdims=True)
            near_column = jnp.sum((table - to_row) * (one - share_row), axis=1, keepdims=True)
            near_row = jnp.sum((table - to_column) * (one - share_column), axis=0, keepdims=True)
            dist_row = jnp.sqrt(jnp.maximum(near_row, 0.0) + 1e-06)
            dist_column = jnp.sqrt(jnp.maximum(near_column, 0.0) + 1e-06)
            weight_row = jnp.where(in_row, 1.0 / dist_row, 0.0)
            weight_column = jnp.where(in_column, 1.0 / dist_column, 0.0)
            share_row = weight_row / jnp.sum(weight_row)
            share_column = weight_column / jnp.sum(weight_column)
        mine = share_row * factor_ref[...]
        lanes = lax.broadcasted_iota(jnp.int32, (1, shape[1]), 1)
        for k in range(count):
            coef[k] = jnp.sum(jnp.where(lanes == slots_ref[k], mine, 0.0))

    scales = [coef[k] for k in range(count)]
    rows = gate_out.shape[0]
    chunk = 16
    for matrix, out in ((0, gate_out), (1, up_out)):

        def body(at, carry, matrix=matrix, out=out):
            span = pl.ds(pl.multiple_of(at * chunk, chunk), chunk)
            total = scales[0] * grads[0][matrix, span, :].astype(jnp.float32)
            for k in range(1, count):
                total = total + scales[k] * grads[k][matrix, span, :].astype(jnp.float32)
            out[span, :] = total
            return carry

        lax.fori_loop(0, rows // chunk, body, 0)


def on_device(order, hidden_states, norm_gain, gate_weight, up_weight, hidden_grad, byz_order, byz_scale):
    count, shards = len(order), lax.axis_size("fsdp")
    colony, shard = lax.axis_index("colony"), lax.axis_index("fsdp")
    width = gate_weight.shape[1]
    depth = hidden_states.shape[2]
    share = hidden_states.shape[1]
    half = share // 2
    rows = depth // count
    total_tokens = share * shards
    block = 256 if width % 256 == 0 else 128
    place = {c: at for at, c in enumerate(order)}
    shifts = slot_shifts(count)

    def hop(value, delta):
        pairs = []
        for c in range(count):
            to = order[(place[c] + delta) % count]
            pairs.append((c, to))
        return lax.ppermute(value, "colony", pairs)

    def swap(value, mask):
        return lax.ppermute(value, "fsdp", [(j, j ^ mask) for j in range(shards)])

    def spread_chips(own):
        pieces = {0: own}
        bit = shards // 2
        while bit > 1:
            for m in list(pieces):
                pieces[m | bit] = swap(pieces[m], bit)
            bit //= 2
        return pieces

    def spread_cores(pieces):
        every = dict(pieces)
        for m, piece in pieces.items():
            every[m | 1] = swap(piece, 1)
        return [every[m] for m in range(shards)]

    values = hidden_states[0].astype(jnp.float32)
    meansq = jnp.mean(values * values, axis=-1, keepdims=True)
    normed = (values * lax.rsqrt(meansq + 1e-05) * norm_gain).astype(jnp.bfloat16)

    local_grad = hidden_grad[0]
    cuts = []
    for m in range(shards):
        columns = lax.dynamic_slice(local_grad, (0, (shard ^ m) * width), (share, width))
        cuts.append(columns if m == 0 else swap(columns, m))
    cot = jnp.concatenate([c[h * half : (h + 1) * half] for h in range(2) for c in cuts], axis=0)
    mid = total_tokens // 2

    ring = jnp.asarray(order, jnp.int32)
    at = jnp.asarray([place[c] for c in range(count)], jnp.int32)[colony]
    held = ring[(at - jnp.asarray(shifts, jnp.int32)) % count]
    slots = jnp.concatenate([held, colony[None].astype(jnp.int32)])
    table_shape = (max(8, count), 128)
    lanes = jnp.arange(128, dtype=jnp.int32)
    hits = byz_order[:NBYZ][:, None] == lanes[None, :]
    factor = 1.0 + jnp.sum(jnp.where(hits, -byz_scale[:, None] - 1.0, jnp.float32(0.0)), axis=0)
    factor = jnp.where(lanes < count, factor, 0.0)
    factors = factor[: table_shape[0], None] * factor[None, :]

    smem = pl.BlockSpec(memory_space=pltpu.SMEM)
    anywhere = pl.BlockSpec(memory_space=pl.ANY)
    column = pl.BlockSpec((depth, block), lambda b: (0, b))
    block_of_grad = pl.BlockSpec((2, rows, block), lambda b: (0, 0, b))

    def colonies(group, tokens, cots, before):
        if n_pieces := len(cots[0]) - 1:
            parts = [
                [(m, h * half, half, (h * shards + m) * half) for h in range(2) for m in range(shards)]
            ]
        else:
            parts = [
                [
                    (m, at * share + h * half, half, (h * shards + m) * half)
                    for h in range(2)
                    for m in range(shards)
                ]
                for at in range(len(group))
            ]
        n_cot = n_pieces + 1
        last = group[-1] == count - 1
        in_specs = [smem] + [anywhere] * shards + [column, column]
        in_specs += [pl.BlockSpec((c.shape[0], block), lambda b: (0, b)) for c in sum(cots, [])]
        out_shape = [jax.ShapeDtypeStruct((2, rows, width), jnp.bfloat16)] * len(group)
        out_specs = [block_of_grad] * len(group)
        scratch = [
            pltpu.VMEM((len(group), total_tokens, depth), jnp.bfloat16),
            pltpu.VMEM((len(group), rows, total_tokens), jnp.bfloat16),
            pltpu.SemaphoreType.DMA((len(group), 2 * shards)),
        ]
        operands = [slots, *tokens, gate_weight, up_weight, *sum(cots, [])]
        if last:
            in_specs += [block_of_grad] * len(before)
            operands += before
            out_shape.append(jax.ShapeDtypeStruct(table_shape, jnp.float32))
            out_specs.append(pl.BlockSpec(table_shape, lambda b: (0, 0)))
            scratch.append(pltpu.VMEM((256, 256), jnp.float32))
        flops = len(group) * 2 * total_tokens * width * 2 * (depth + rows)
        return pl.pallas_call(
            functools.partial(colony_kernel, group, count, parts, shards, n_cot),
            grid=(width // block,),
            in_specs=in_specs,
            out_specs=out_specs,
            out_shape=out_shape,
            scratch_shapes=scratch,
            compiler_params=pltpu.CompilerParams(vmem_limit_bytes=VMEM),
            cost_estimate=pl.CostEstimate(
                flops=flops, bytes_accessed=4 * depth * width, transcendentals=total_tokens * width
            ),
        )(*operands)

    ways = (1, -1)
    far = count // 2
    n_at = {(0, way): normed for way in ways}
    c_at = {(0, way): cot for way in ways}

    def send_tokens(step):
        for h, way in enumerate(ways):
            value = n_at[step - 1, way]
            if step == far:
                value = value[h * half : (h + 1) * half]
            n_at[step, way] = hop(value, way)

    def send_cot(step):
        for h, way in enumerate(ways):
            value = c_at[step - 1, way]
            if step == far:
                value = value[h * mid : (h + 1) * mid]
            c_at[step, way] = hop(value, way)

    def both(step):
        return jnp.concatenate([n_at[step, way] for way in ways], axis=0)

    def fence():
        nonlocal n_at, c_at, chips, grads
        n_at, c_at, chips, grads = lax.optimization_barrier((n_at, c_at, chips, grads))

    grads, chips = [], {0: normed}
    send_tokens(1)
    fence()
    chips[0] = spread_chips(chips[0])
    send_tokens(2)
    fence()
    for step in range(far + 1):
        cores = spread_cores(chips[step])
        if step + 1 <= far:
            send_cot(step + 1)
            chips[step + 1] = spread_chips(both(step + 1))
        if 0 < step <= far - 2:
            send_tokens(step + 2)
        if step == 0:
            group, cots = [0], [[c_at[0, 1]]]
        elif step < far:
            group, cots = [2 * step - 1, 2 * step], [[c_at[step, way]] for way in ways]
        else:
            group, cots = [count - 1], [[c_at[far, way] for way in ways]]
        grads = [*grads, *colonies(group, cores, cots, grads)]
        if step < far:
            fence()
    table = grads.pop()
    devices = count * shards
    bit = 1
    while bit < devices:
        table = table + lax.ppermute(table, AXES, [(d, d ^ bit) for d in range(devices)])
        bit *= 2

    cut = min(64, rows)
    whole = pl.BlockSpec(table_shape, lambda b: (0, 0))
    out_block = pl.BlockSpec((cut, width), lambda b: (b, 0))
    return pl.pallas_call(
        functools.partial(combine_kernel, count),
        grid=(rows // cut,),
        in_specs=[whole, whole, pl.BlockSpec((1, 128), lambda b: (0, 0)), smem]
        + [pl.BlockSpec((2, cut, width), lambda b: (0, b, 0))] * count,
        out_specs=[out_block, out_block],
        out_shape=[jax.ShapeDtypeStruct((rows, width), jnp.float32)] * 2,
        scratch_shapes=[pltpu.SMEM((count,), jnp.float32)],
        compiler_params=pltpu.CompilerParams(vmem_limit_bytes=VMEM),
    )(table, factors, factor[None], slots, *grads)


def solution(mesh):
    placed = (
        P("colony", "fsdp", None),
        P(),
        P(None, "fsdp"),
        P(None, "fsdp"),
        P("colony", "fsdp", None),
        P(),
        P(),
    )
    return jax.shard_map(
        functools.partial(on_device, ring_order(mesh.shape["colony"])),
        mesh=mesh,
        in_specs=placed,
        out_specs=(P("colony", "fsdp"), P("colony", "fsdp")),
        check_vma=False,
    )
```

```python
import functools

import jax
import jax.numpy as jnp
from jax import lax
from jax.experimental import pallas as pl
from jax.experimental.pallas import tpu as pltpu
from jax.sharding import PartitionSpec as P

NBYZ = 3
ITERS = 3
LINE = 4
AXES = ("colony", "fsdp")
VMEM = 28 * 1024 * 1024
VMEM_FIRST = 50 * 1024 * 1024


def ring_order(count):
    width = count // LINE
    if count % LINE or width % 2:
        return list(range(count))
    order = [(0, 0)]
    for y in range(width):
        column = list(range(1, LINE))
        order += [(z, y) for z in (column if y % 2 == 0 else column[::-1])]
    order += [(0, y) for y in range(width - 1, 0, -1)]
    return [z * width + y for z, y in order]


def slot_shifts(count):
    shifts = [0]
    for step in range(1, count // 2):
        shifts += [step, -step]
    return shifts + [count // 2]


def exact_dot(left, right):
    return jnp.dot(
        left, right, precision=lax.Precision.HIGHEST, preferred_element_type=jnp.float32
    )


def one_hot(shape, axis, sub, slots_ref, slots):
    piece = lax.broadcasted_iota(jnp.int32, shape, axis)
    colony = lax.broadcasted_iota(jnp.int32, shape, 1 - axis)
    result = jnp.zeros(shape, jnp.float32)
    for slot in slots:
        hit = (piece >= slot * sub) & (piece < (slot + 1) * sub) & (colony == slots_ref[slot])
        result = jnp.where(hit, 1.0, result)
    return result


def colony_kernel(slots, count, parts, n_parts, n_cot, *refs):
    refs = list(refs)
    last = slots[-1] == count - 1
    slots_ref = refs.pop(0)
    parts_refs = [refs.pop(0) for _ in range(n_parts)]
    gate_ref, up_ref = refs.pop(0), refs.pop(0)
    cot_refs = [[refs.pop(0) for _ in range(n_cot)] for _ in slots]
    before = [refs.pop(0) for _ in range(slots[0])] if last else []
    grad_refs = [refs.pop(0) for _ in slots]
    table_ref = refs.pop(0) if last else None
    tokens, rows_t, sems = refs[:3]
    gram = refs[3] if last else None
    step = pl.program_id(0)
    rows = rows_t.shape[1]

    copies = []
    for at, part in enumerate(parts):
        copies.append([])
        for which, start, size, target in part:
            copies[at].append(
                pltpu.make_async_copy(
                    parts_refs[which].at[pl.ds(start, size)],
                    tokens.at[at, pl.ds(target, size)],
                    sems.at[at, len(copies[at])],
                )
            )

    def arrive(at):
        for copy in copies[at]:
            copy.wait()
        if at + 1 < len(slots):
            for copy in copies[at + 1]:
                copy.start()
        first = pl.multiple_of(slots_ref[count] * rows, rows)
        rows_t[at] = tokens[at, :, pl.ds(first, rows)].T

    def gradients(at):
        gate = jnp.dot(tokens[at], gate_ref[...], preferred_element_type=jnp.float32)
        up = jnp.dot(tokens[at], up_ref[...], preferred_element_type=jnp.float32)
        sig = jax.nn.sigmoid(gate)
        cot = [ref[...] for ref in cot_refs[at]]
        back = (cot[0] if n_cot == 1 else jnp.concatenate(cot, axis=0)).astype(jnp.float32)
        d_up = (back * gate * sig).astype(jnp.bfloat16)
        d_gate = (back * up * sig * (1.0 + gate * (1.0 - sig))).astype(jnp.bfloat16)
        for matrix, delta in ((0, d_gate), (1, d_up)):
            grad_refs[at][matrix] = jnp.dot(
                rows_t[at], delta, preferred_element_type=jnp.float32
            ).astype(jnp.bfloat16)

    def products():
        every = before + grad_refs
        sub = gram.shape[0] // count
        wide = 8

        def add(at, carry):
            cut = []
            for part in range(wide):
                span = pl.ds(pl.multiple_of((at * wide + part) * sub, sub), sub)
                for matrix in range(2):
                    pieces = [ref[matrix, span, :] for ref in every]
                    cut.append(jnp.concatenate(pieces, axis=0))
            side = jnp.concatenate(cut, axis=1)
            gram[...] += lax.dot_general(
                side, side, (((1,), (1,)), ((), ())), preferred_element_type=jnp.float32
            )
            return carry

        lax.fori_loop(0, rows // (sub * wide), add, 0)

    @pl.when(step == 0)
    def _():
        for copy in copies[0]:
            copy.start()
        if last:
            gram[...] = jnp.zeros_like(gram)
        for at in range(len(slots)):
            arrive(at)
            gradients(at)

    @pl.when(step > 0)
    def _():
        for at in range(len(slots)):
            gradients(at)

    if last:
        products()

        @pl.when(step == pl.num_programs(0) - 1)
        def _():
            size = gram.shape[0]
            sub = size // count
            row = lax.broadcasted_iota(jnp.int32, gram.shape, 0)
            lane = lax.broadcasted_iota(jnp.int32, gram.shape, 1)
            kept = jnp.where((row & (sub - 1)) == (lane & (sub - 1)), gram[...], 0.0)
            left = one_hot((table_ref.shape[0], size), 1, sub, slots_ref, range(count))
            right = one_hot((size, table_ref.shape[1]), 0, sub, slots_ref, range(count))
            table_ref[...] = exact_dot(exact_dot(left, kept), right)


def combine_kernel(count, table_ref, factors_ref, factor_ref, slots_ref, *refs):
    grads = refs[:count]
    gate_out, up_out = refs[count : count + 2]
    coef = refs[count + 2]

    @pl.when(pl.program_id(0) == 0)
    def _():
        table = table_ref[...] * factors_ref[...]
        shape = table.shape
        row = lax.broadcasted_iota(jnp.int32, shape, 0)
        lane = lax.broadcasted_iota(jnp.int32, shape, 1)
        one = jnp.where(row == lane, 1.0, 0.0)
        in_row = lax.broadcasted_iota(jnp.int32, (1, shape[1]), 1) < count
        in_column = lax.broadcasted_iota(jnp.int32, (shape[0], 1), 0) < count
        share_row = jnp.where(in_row, 1.0 / count, 0.0)
        share_column = jnp.where(in_column, 1.0 / count, 0.0)
        for _ in range(ITERS):
            to_row = jnp.sum(table * share_column, axis=0, keepdims=True)
            to_column = jnp.sum(table * share_row, axis=1, keepdims=True)
            near_column = jnp.sum((table - to_row) * (one - share_row), axis=1, keepdims=True)
            near_row = jnp.sum((table - to_column) * (one - share_column), axis=0, keepdims=True)
            dist_row = jnp.sqrt(jnp.maximum(near_row, 0.0) + 1e-06)
            dist_column = jnp.sqrt(jnp.maximum(near_column, 0.0) + 1e-06)
            weight_row = jnp.where(in_row, 1.0 / dist_row, 0.0)
            weight_column = jnp.where(in_column, 1.0 / dist_column, 0.0)
            share_row = weight_row / jnp.sum(weight_row)
            share_column = weight_column / jnp.sum(weight_column)
        mine = share_row * factor_ref[...]
        lanes = lax.broadcasted_iota(jnp.int32, (1, shape[1]), 1)
        for k in range(count):
            coef[k] = jnp.sum(jnp.where(lanes == slots_ref[k], mine, 0.0))

    scales = [coef[k] for k in range(count)]
    rows = gate_out.shape[0]
    chunk = 16
    for matrix, out in ((0, gate_out), (1, up_out)):

        def body(at, carry, matrix=matrix, out=out):
            span = pl.ds(pl.multiple_of(at * chunk, chunk), chunk)
            total = scales[0] * grads[0][matrix, span, :].astype(jnp.float32)
            for k in range(1, count):
                total = total + scales[k] * grads[k][matrix, span, :].astype(jnp.float32)
            out[span, :] = total
            return carry

        lax.fori_loop(0, rows // chunk, body, 0)


def on_device(order, hidden_states, norm_gain, gate_weight, up_weight, hidden_grad, byz_order, byz_scale):
    count, shards = len(order), lax.axis_size("fsdp")
    colony, shard = lax.axis_index("colony"), lax.axis_index("fsdp")
    width = gate_weight.shape[1]
    depth = hidden_states.shape[2]
    share = hidden_states.shape[1]
    half = share // 2
    rows = depth // count
    total_tokens = share * shards
    block = 256 if width % 256 == 0 else 128
    place = {c: at for at, c in enumerate(order)}
    shifts = slot_shifts(count)

    def hop(value, delta):
        pairs = []
        for c in range(count):
            to = order[(place[c] + delta) % count]
            pairs.append((c, to))
        return lax.ppermute(value, "colony", pairs)

    def swap(value, mask):
        return lax.ppermute(value, "fsdp", [(j, j ^ mask) for j in range(shards)])

    def spread_chips(own):
        pieces = {0: own}
        bit = shards // 2
        while bit > 1:
            for m in list(pieces):
                pieces[m | bit] = swap(pieces[m], bit)
            bit //= 2
        return pieces

    def spread_cores(pieces):
        every = dict(pieces)
        for m, piece in pieces.items():
            every[m | 1] = swap(piece, 1)
        return [every[m] for m in range(shards)]

    values = hidden_states[0].astype(jnp.float32)
    meansq = jnp.mean(values * values, axis=-1, keepdims=True)
    normed = (values * lax.rsqrt(meansq + 1e-05) * norm_gain).astype(jnp.bfloat16)

    local_grad = hidden_grad[0]
    cuts = []
    for m in range(shards):
        columns = lax.dynamic_slice(local_grad, (0, (shard ^ m) * width), (share, width))
        cuts.append(columns if m == 0 else swap(columns, m))
    cot = jnp.concatenate([c[h * half : (h + 1) * half] for h in range(2) for c in cuts], axis=0)
    mid = total_tokens // 2

    ring = jnp.asarray(order, jnp.int32)
    at = jnp.asarray([place[c] for c in range(count)], jnp.int32)[colony]
    held = ring[(at - jnp.asarray(shifts, jnp.int32)) % count]
    slots = jnp.concatenate([held, colony[None].astype(jnp.int32)])
    table_shape = (max(8, count), 128)
    lanes = jnp.arange(128, dtype=jnp.int32)
    hits = byz_order[:NBYZ][:, None] == lanes[None, :]
    factor = 1.0 + jnp.sum(jnp.where(hits, -byz_scale[:, None] - 1.0, jnp.float32(0.0)), axis=0)
    factor = jnp.where(lanes < count, factor, 0.0)
    factors = factor[: table_shape[0], None] * factor[None, :]

    smem = pl.BlockSpec(memory_space=pltpu.SMEM)
    main = pl.BlockSpec(memory_space=pltpu.HBM)
    column = pl.BlockSpec((depth, block), lambda b: (0, b))
    block_of_grad = pl.BlockSpec((2, rows, block), lambda b: (0, 0, b))

    def colonies(group, tokens, cots, before):
        if n_pieces := len(cots[0]) - 1:
            parts = [
                [(m, h * half, half, (h * shards + m) * half) for h in range(2) for m in range(shards)]
            ]
        else:
            parts = [
                [
                    (m, at * share + h * half, half, (h * shards + m) * half)
                    for h in range(2)
                    for m in range(shards)
                ]
                for at in range(len(group))
            ]
        n_cot = n_pieces + 1
        last = group[-1] == count - 1
        in_specs = [smem] + [main] * shards + [column, column]
        in_specs += [pl.BlockSpec((c.shape[0], block), lambda b: (0, b)) for c in sum(cots, [])]
        out_shape = [jax.ShapeDtypeStruct((2, rows, width), jnp.bfloat16)] * len(group)
        out_specs = [block_of_grad] * len(group)
        scratch = [
            pltpu.VMEM((len(group), total_tokens, depth), jnp.bfloat16),
            pltpu.VMEM((len(group), rows, total_tokens), jnp.bfloat16),
            pltpu.SemaphoreType.DMA((len(group), 2 * shards)),
        ]
        held = functools.partial(pltpu.with_memory_space_constraint, memory_space=pltpu.HBM)
        tokens = [held(piece) for piece in tokens]
        cots = [[held(piece) for piece in pieces] for pieces in cots]
        operands = [slots, *tokens, held(gate_weight), held(up_weight), *sum(cots, [])]
        if last:
            in_specs += [block_of_grad] * len(before)
            operands += before
            out_shape.append(jax.ShapeDtypeStruct(table_shape, jnp.float32))
            out_specs.append(pl.BlockSpec(table_shape, lambda b: (0, 0)))
            scratch.append(pltpu.VMEM((256, 256), jnp.float32))
        flops = len(group) * 2 * total_tokens * width * 2 * (depth + rows)
        return pl.pallas_call(
            functools.partial(colony_kernel, group, count, parts, shards, n_cot),
            grid=(width // block,),
            in_specs=in_specs,
            out_specs=out_specs,
            out_shape=out_shape,
            scratch_shapes=scratch,
            compiler_params=pltpu.CompilerParams(
                vmem_limit_bytes=VMEM if group[0] else VMEM_FIRST
            ),
            cost_estimate=pl.CostEstimate(
                flops=flops, bytes_accessed=4 * depth * width, transcendentals=total_tokens * width
            ),
        )(*operands)

    ways = (1, -1)
    far = count // 2
    n_at = {(0, way): normed for way in ways}
    c_at = {(0, way): cot for way in ways}

    def send_tokens(step):
        for h, way in enumerate(ways):
            value = n_at[step - 1, way]
            if step == far:
                value = value[h * half : (h + 1) * half]
            n_at[step, way] = hop(value, way)

    def send_cot(step):
        for h, way in enumerate(ways):
            value = c_at[step - 1, way]
            if step == far:
                value = value[h * mid : (h + 1) * mid]
            c_at[step, way] = hop(value, way)

    def both(step):
        return jnp.concatenate([n_at[step, way] for way in ways], axis=0)

    def fence():
        nonlocal n_at, c_at, chips, grads, joined
        n_at, c_at, chips, grads, joined = lax.optimization_barrier(
            (n_at, c_at, chips, grads, joined)
        )

    grads, chips, joined = [], {0: normed}, {}
    send_tokens(1)
    fence()
    chips[0] = spread_chips(chips[0])
    send_tokens(2)
    joined[1] = both(1)
    fence()
    for step in range(far + 1):
        cores = spread_cores(chips[step])
        if step + 1 <= far:
            send_cot(step + 1)
            if step + 1 not in joined:
                joined[step + 1] = both(step + 1)
            chips[step + 1] = spread_chips(joined.pop(step + 1))
        if step == 0:
            joined[2] = both(2)
        if 0 < step <= far - 2:
            send_tokens(step + 2)
        if step == 0:
            group, cots = [0], [[c_at[0, 1]]]
        elif step < far:
            group, cots = [2 * step - 1, 2 * step], [[c_at[step, way]] for way in ways]
        else:
            group, cots = [count - 1], [[c_at[far, way] for way in ways]]
        grads = [*grads, *colonies(group, cores, cots, grads)]
        if step < far:
            fence()
    table = grads.pop()
    devices = count * shards
    bit = 1
    while bit < devices:
        table = table + lax.ppermute(table, AXES, [(d, d ^ bit) for d in range(devices)])
        bit *= 2

    cut = min(64, rows)
    whole = pl.BlockSpec(table_shape, lambda b: (0, 0))
    out_block = pl.BlockSpec((cut, width), lambda b: (b, 0))
    return pl.pallas_call(
        functools.partial(combine_kernel, count),
        grid=(rows // cut,),
        in_specs=[whole, whole, pl.BlockSpec((1, 128), lambda b: (0, 0)), smem]
        + [pl.BlockSpec((2, cut, width), lambda b: (0, b, 0))] * count,
        out_specs=[out_block, out_block],
        out_shape=[jax.ShapeDtypeStruct((rows, width), jnp.float32)] * 2,
        scratch_shapes=[pltpu.SMEM((count,), jnp.float32)],
        compiler_params=pltpu.CompilerParams(vmem_limit_bytes=VMEM),
    )(table, factors, factor[None], slots, *grads)


def solution(mesh):
    placed = (
        P("colony", "fsdp", None),
        P(),
        P(None, "fsdp"),
        P(None, "fsdp"),
        P("colony", "fsdp", None),
        P(),
        P(),
    )
    return jax.shard_map(
        functools.partial(on_device, ring_order(mesh.shape["colony"])),
        mesh=mesh,
        in_specs=placed,
        out_specs=(P("colony", "fsdp"), P("colony", "fsdp")),
        check_vma=False,
    )
```

```python
import functools

import jax
import jax.numpy as jnp
from jax import lax
from jax.experimental import pallas as pl
from jax.experimental.pallas import tpu as pltpu
from jax.sharding import PartitionSpec as P

NBYZ = 3
ITERS = 3
LINE = 4
AXES = ("colony", "fsdp")
VMEM = 24 * 1024 * 1024
VMEM_FIRST = 50 * 1024 * 1024


def ring_order(count):
    width = count // LINE
    if count % LINE or width % 2:
        return list(range(count))
    order = [(0, 0)]
    for y in range(width):
        column = list(range(1, LINE))
        order += [(z, y) for z in (column if y % 2 == 0 else column[::-1])]
    order += [(0, y) for y in range(width - 1, 0, -1)]
    return [z * width + y for z, y in order]


def slot_shifts(count):
    shifts = [0]
    for step in range(1, count // 2):
        shifts += [step, -step]
    return shifts + [count // 2]


def exact_dot(left, right):
    return jnp.dot(
        left, right, precision=lax.Precision.HIGHEST, preferred_element_type=jnp.float32
    )


def one_hot(shape, axis, sub, slots_ref, slots):
    piece = lax.broadcasted_iota(jnp.int32, shape, axis)
    colony = lax.broadcasted_iota(jnp.int32, shape, 1 - axis)
    result = jnp.zeros(shape, jnp.float32)
    for slot in slots:
        hit = (piece >= slot * sub) & (piece < (slot + 1) * sub) & (colony == slots_ref[slot])
        result = jnp.where(hit, 1.0, result)
    return result


def colony_kernel(slots, count, parts, n_parts, n_cot, *refs):
    refs = list(refs)
    last = slots[-1] == count - 1
    slots_ref = refs.pop(0)
    parts_refs = [refs.pop(0) for _ in range(n_parts)]
    gate_ref, up_ref = refs.pop(0), refs.pop(0)
    cot_refs = [[refs.pop(0) for _ in range(n_cot)] for _ in slots]
    before = [refs.pop(0) for _ in range(slots[0])] if last else []
    grad_refs = [refs.pop(0) for _ in slots]
    table_ref = refs.pop(0) if last else None
    tokens, rows_t, sems = refs[:3]
    gram = refs[3] if last else None
    step = pl.program_id(0)
    rows = rows_t.shape[1]

    copies = []
    for at, part in enumerate(parts):
        copies.append([])
        for which, start, size, target in part:
            copies[at].append(
                pltpu.make_async_copy(
                    parts_refs[which].at[pl.ds(start, size)],
                    tokens.at[at, pl.ds(target, size)],
                    sems.at[at, len(copies[at])],
                )
            )

    def arrive(at):
        for copy in copies[at]:
            copy.wait()
        if at + 1 < len(slots):
            for copy in copies[at + 1]:
                copy.start()
        first = pl.multiple_of(slots_ref[count] * rows, rows)
        rows_t[at] = tokens[at, :, pl.ds(first, rows)].T

    def gradients(at):
        gate = jnp.dot(tokens[at], gate_ref[...], preferred_element_type=jnp.float32)
        up = jnp.dot(tokens[at], up_ref[...], preferred_element_type=jnp.float32)
        sig = jax.nn.sigmoid(gate)
        cot = [ref[...] for ref in cot_refs[at]]
        back = (cot[0] if n_cot == 1 else jnp.concatenate(cot, axis=0)).astype(jnp.float32)
        d_up = (back * gate * sig).astype(jnp.bfloat16)
        d_gate = (back * up * sig * (1.0 + gate * (1.0 - sig))).astype(jnp.bfloat16)
        for matrix, delta in ((0, d_gate), (1, d_up)):
            grad_refs[at][matrix] = jnp.dot(
                rows_t[at], delta, preferred_element_type=jnp.float32
            ).astype(jnp.bfloat16)

    def products():
        every = before + grad_refs
        sub = gram.shape[0] // count
        wide = 8

        def add(at, carry):
            cut = []
            for part in range(wide):
                span = pl.ds(pl.multiple_of((at * wide + part) * sub, sub), sub)
                for matrix in range(2):
                    pieces = [ref[matrix, span, :] for ref in every]
                    cut.append(jnp.concatenate(pieces, axis=0))
            side = jnp.concatenate(cut, axis=1)
            gram[...] += lax.dot_general(
                side, side, (((1,), (1,)), ((), ())), preferred_element_type=jnp.float32
            )
            return carry

        lax.fori_loop(0, rows // (sub * wide), add, 0)

    @pl.when(step == 0)
    def _():
        for copy in copies[0]:
            copy.start()
        if last:
            gram[...] = jnp.zeros_like(gram)
        for at in range(len(slots)):
            arrive(at)
            gradients(at)

    @pl.when(step > 0)
    def _():
        for at in range(len(slots)):
            gradients(at)

    if last:
        products()

        @pl.when(step == pl.num_programs(0) - 1)
        def _():
            size = gram.shape[0]
            sub = size // count
            row = lax.broadcasted_iota(jnp.int32, gram.shape, 0)
            lane = lax.broadcasted_iota(jnp.int32, gram.shape, 1)
            kept = jnp.where((row & (sub - 1)) == (lane & (sub - 1)), gram[...], 0.0)
            left = one_hot((table_ref.shape[0], size), 1, sub, slots_ref, range(count))
            right = one_hot((size, table_ref.shape[1]), 0, sub, slots_ref, range(count))
            table_ref[...] = exact_dot(exact_dot(left, kept), right)


def combine_kernel(count, table_ref, factors_ref, factor_ref, slots_ref, *refs):
    grads = refs[:count]
    gate_out, up_out = refs[count : count + 2]
    coef, held, sems = refs[count + 2 :]

    def weigh():
        table = table_ref[...] * factors_ref[...]
        shape = table.shape
        row = lax.broadcasted_iota(jnp.int32, shape, 0)
        lane = lax.broadcasted_iota(jnp.int32, shape, 1)
        one = jnp.where(row == lane, 1.0, 0.0)
        in_row = lax.broadcasted_iota(jnp.int32, (1, shape[1]), 1) < count
        in_column = lax.broadcasted_iota(jnp.int32, (shape[0], 1), 0) < count
        share_row = jnp.where(in_row, 1.0 / count, 0.0)
        share_column = jnp.where(in_column, 1.0 / count, 0.0)
        for _ in range(ITERS):
            to_row = jnp.sum(table * share_column, axis=0, keepdims=True)
            to_column = jnp.sum(table * share_row, axis=1, keepdims=True)
            near_column = jnp.sum((table - to_row) * (one - share_row), axis=1, keepdims=True)
            near_row = jnp.sum((table - to_column) * (one - share_column), axis=0, keepdims=True)
            dist_row = jnp.sqrt(jnp.maximum(near_row, 0.0) + 1e-06)
            dist_column = jnp.sqrt(jnp.maximum(near_column, 0.0) + 1e-06)
            weight_row = jnp.where(in_row, 1.0 / dist_row, 0.0)
            weight_column = jnp.where(in_column, 1.0 / dist_column, 0.0)
            share_row = weight_row / jnp.sum(weight_row)
            share_column = weight_column / jnp.sum(weight_column)
        mine = share_row * factor_ref[...]
        lanes = lax.broadcasted_iota(jnp.int32, (1, shape[1]), 1)
        for k in range(count):
            coef[k] = jnp.sum(jnp.where(lanes == slots_ref[k], mine, 0.0))

    weigh()
    scales = [coef[k] for k in range(count)]
    rows = gate_out.shape[0]
    slots, cut, chunk = held.shape[0], held.shape[1], 16
    copies = []
    for first in range(0, rows, cut):
        for matrix, out in ((0, gate_out), (1, up_out)):
            slot = len(copies) % slots
            if len(copies) >= slots:
                copies[-slots].wait()

            def body(at, carry, matrix=matrix, first=first, slot=slot):
                start = pl.multiple_of(at * chunk, chunk)
                span = pl.ds(first + start, chunk)
                total = scales[0] * grads[0][matrix, span, :].astype(jnp.float32)
                for k in range(1, count):
                    total = total + scales[k] * grads[k][matrix, span, :].astype(jnp.float32)
                held[slot, pl.ds(start, chunk), :] = total
                return carry

            lax.fori_loop(0, cut // chunk, body, 0)
            copy = pltpu.make_async_copy(
                held.at[slot], out.at[pl.ds(first, cut)], sems.at[slot]
            )
            copy.start()
            copies.append(copy)
    for copy in copies[-slots:]:
        copy.wait()


def on_device(order, hidden_states, norm_gain, gate_weight, up_weight, hidden_grad, byz_order, byz_scale):
    count, shards = len(order), lax.axis_size("fsdp")
    colony, shard = lax.axis_index("colony"), lax.axis_index("fsdp")
    width = gate_weight.shape[1]
    depth = hidden_states.shape[2]
    share = hidden_states.shape[1]
    half = share // 2
    rows = depth // count
    total_tokens = share * shards
    block = 256 if width % 256 == 0 else 128
    place = {c: at for at, c in enumerate(order)}
    shifts = slot_shifts(count)

    def hop(value, delta):
        pairs = []
        for c in range(count):
            to = order[(place[c] + delta) % count]
            pairs.append((c, to))
        return lax.ppermute(value, "colony", pairs)

    def swap(value, mask):
        return lax.ppermute(value, "fsdp", [(j, j ^ mask) for j in range(shards)])

    def spread_chips(own):
        pieces = {0: own}
        bit = shards // 2
        while bit > 1:
            for m in list(pieces):
                pieces[m | bit] = swap(pieces[m], bit)
            bit //= 2
        return pieces

    def spread_cores(pieces):
        every = dict(pieces)
        for m, piece in pieces.items():
            every[m | 1] = swap(piece, 1)
        return [every[m] for m in range(shards)]

    values = hidden_states[0].astype(jnp.float32)
    meansq = jnp.mean(values * values, axis=-1, keepdims=True)
    normed = (values * lax.rsqrt(meansq + 1e-05) * norm_gain).astype(jnp.bfloat16)

    local_grad = hidden_grad[0]
    cuts = []
    for m in range(shards):
        columns = lax.dynamic_slice(local_grad, (0, (shard ^ m) * width), (share, width))
        cuts.append(columns if m == 0 else swap(columns, m))
    cot = jnp.concatenate([c[h * half : (h + 1) * half] for h in range(2) for c in cuts], axis=0)
    mid = total_tokens // 2

    ring = jnp.asarray(order, jnp.int32)
    at = jnp.asarray([place[c] for c in range(count)], jnp.int32)[colony]
    held = ring[(at - jnp.asarray(shifts, jnp.int32)) % count]
    slots = jnp.concatenate([held, colony[None].astype(jnp.int32)])
    table_shape = (max(8, count), 128)
    lanes = jnp.arange(128, dtype=jnp.int32)
    hits = byz_order[:NBYZ][:, None] == lanes[None, :]
    factor = 1.0 + jnp.sum(jnp.where(hits, -byz_scale[:, None] - 1.0, jnp.float32(0.0)), axis=0)
    factor = jnp.where(lanes < count, factor, 0.0)
    factors = factor[: table_shape[0], None] * factor[None, :]

    smem = pl.BlockSpec(memory_space=pltpu.SMEM)
    main = pl.BlockSpec(memory_space=pltpu.HBM)
    column = pl.BlockSpec((depth, block), lambda b: (0, b))
    block_of_grad = pl.BlockSpec((2, rows, block), lambda b: (0, 0, b))

    def colonies(group, tokens, cots, before):
        if n_pieces := len(cots[0]) - 1:
            parts = [
                [(m, h * half, half, (h * shards + m) * half) for h in range(2) for m in range(shards)]
            ]
        else:
            parts = [
                [
                    (m, at * share + h * half, half, (h * shards + m) * half)
                    for h in range(2)
                    for m in range(shards)
                ]
                for at in range(len(group))
            ]
        n_cot = n_pieces + 1
        last = group[-1] == count - 1
        in_specs = [smem] + [main] * shards + [column, column]
        in_specs += [pl.BlockSpec((c.shape[0], block), lambda b: (0, b)) for c in sum(cots, [])]
        out_shape = [jax.ShapeDtypeStruct((2, rows, width), jnp.bfloat16)] * len(group)
        out_specs = [block_of_grad] * len(group)
        scratch = [
            pltpu.VMEM((len(group), total_tokens, depth), jnp.bfloat16),
            pltpu.VMEM((len(group), rows, total_tokens), jnp.bfloat16),
            pltpu.SemaphoreType.DMA((len(group), 2 * shards)),
        ]
        held = functools.partial(pltpu.with_memory_space_constraint, memory_space=pltpu.HBM)
        tokens = [held(piece) for piece in tokens]
        cots = [[held(piece) for piece in pieces] for pieces in cots]
        operands = [slots, *tokens, held(gate_weight), held(up_weight), *sum(cots, [])]
        if last:
            in_specs += [block_of_grad] * len(before)
            operands += before
            out_shape.append(jax.ShapeDtypeStruct(table_shape, jnp.float32))
            out_specs.append(pl.BlockSpec(table_shape, lambda b: (0, 0)))
            scratch.append(pltpu.VMEM((256, 256), jnp.float32))
        flops = len(group) * 2 * total_tokens * width * 2 * (depth + rows)
        return pl.pallas_call(
            functools.partial(colony_kernel, group, count, parts, shards, n_cot),
            grid=(width // block,),
            in_specs=in_specs,
            out_specs=out_specs,
            out_shape=out_shape,
            scratch_shapes=scratch,
            compiler_params=pltpu.CompilerParams(
                vmem_limit_bytes=VMEM if group[0] else VMEM_FIRST
            ),
            cost_estimate=pl.CostEstimate(
                flops=flops, bytes_accessed=4 * depth * width, transcendentals=total_tokens * width
            ),
        )(*operands)

    ways = (1, -1)
    far = count // 2
    n_at = {(0, way): normed for way in ways}
    c_at = {(0, way): cot for way in ways}

    def send_tokens(step):
        for h, way in enumerate(ways):
            value = n_at[step - 1, way]
            if step == far:
                value = value[h * half : (h + 1) * half]
            n_at[step, way] = hop(value, way)

    def send_cot(step):
        for h, way in enumerate(ways):
            value = c_at[step - 1, way]
            if step == far:
                value = value[h * mid : (h + 1) * mid]
            c_at[step, way] = hop(value, way)

    def both(step):
        return jnp.concatenate([n_at[step, way] for way in ways], axis=0)

    def fence():
        nonlocal n_at, c_at, chips, grads, joined
        n_at, c_at, chips, grads, joined = lax.optimization_barrier(
            (n_at, c_at, chips, grads, joined)
        )

    grads, chips, joined = [], {0: normed}, {}
    send_tokens(1)
    fence()
    chips[0] = spread_chips(chips[0])
    send_tokens(2)
    joined[1] = both(1)
    fence()
    for step in range(far + 1):
        cores = spread_cores(chips[step])
        if step + 1 <= far:
            send_cot(step + 1)
            if step + 1 not in joined:
                joined[step + 1] = both(step + 1)
            chips[step + 1] = spread_chips(joined.pop(step + 1))
        if step == 0:
            joined[2] = both(2)
        if 0 < step <= far - 2:
            send_tokens(step + 2)
        if step == 0:
            group, cots = [0], [[c_at[0, 1]]]
        elif step < far:
            group, cots = [2 * step - 1, 2 * step], [[c_at[step, way]] for way in ways]
        else:
            group, cots = [count - 1], [[c_at[far, way] for way in ways]]
        grads = [*grads, *colonies(group, cores, cots, grads)]
        if step < far:
            fence()
    table = grads.pop()
    devices = count * shards
    bit = 1
    while bit < devices:
        table = table + lax.ppermute(table, AXES, [(d, d ^ bit) for d in range(devices)])
        bit *= 2

    cut = min(64, rows)
    vmem = pl.BlockSpec(memory_space=pltpu.VMEM)
    main = pl.BlockSpec(memory_space=pltpu.HBM)
    near = [pltpu.with_memory_space_constraint(grad, pltpu.VMEM) for grad in grads]
    return pl.pallas_call(
        functools.partial(combine_kernel, count),
        in_specs=[vmem, vmem, vmem, smem] + [vmem] * count,
        out_specs=[main, main],
        out_shape=[jax.ShapeDtypeStruct((rows, width), jnp.float32)] * 2,
        scratch_shapes=[
            pltpu.SMEM((count,), jnp.float32),
            pltpu.VMEM((4, cut, width), jnp.float32),
            pltpu.SemaphoreType.DMA((4,)),
        ],
        compiler_params=pltpu.CompilerParams(vmem_limit_bytes=VMEM),
    )(table, factors, factor[None], slots, *near)


def solution(mesh):
    placed = (
        P("colony", "fsdp", None),
        P(),
        P(None, "fsdp"),
        P(None, "fsdp"),
        P("colony", "fsdp", None),
        P(),
        P(),
    )
    return jax.shard_map(
        functools.partial(on_device, ring_order(mesh.shape["colony"])),
        mesh=mesh,
        in_specs=placed,
        out_specs=(P("colony", "fsdp"), P("colony", "fsdp")),
        check_vma=False,
    )
```
